32 devices in a mesh: groups: 2 (over y), gx: 4 (over z), gy: 2 (over x), gz: 2 (over core).
Axes of the slice: x: 2, y: 2, z: 4, core: 2. Of those that a mesh axis runs over, the one named last changes fastest.
Arguments:
- stream: float32 [256, 64, 512], P('groups', 'gx', 'gy'), parts along dimension 0, may hold values from -6 to 6
- inductance: bfloat16 [16, 32, 8, 2, 128, 128], P(('groups', 'gx'), ('gy', 'gz')), parts along dimension 0, may hold values from -0.25 to 1.25
- near_lists: int32 [16, 32, 8], P(('groups', 'gx'), ('gy', 'gz')), parts along dimension 0, may hold values from 0 to 8, as said below
- filament_leaf: int32 [16384], P(('groups', 'gx', 'gy', 'gz')), parts along dimension 0, may hold values from 0 to 255, as said below
- filament_current: bfloat16 [16384, 128], P(('groups', 'gx', 'gy', 'gz')), parts along dimension 0, may hold values from -6 to 6
- filament_coupling: bfloat16 [16384, 2, 128], P(('groups', 'gx', 'gy', 'gz')), parts along dimension 0, may hold values from -0.75 to 0.75
Outputs:
- loop_voltage: float32 [256, 64, 512], P('groups', 'gx', ('gy', 'gz')), parts along dimension 0
- filament_voltage: bfloat16 [16384, 128], P(('groups', 'gx', 'gy', 'gz')), parts along dimension 0
The draws below stay inside these ranges and needn't reach their ends.
There are 2 independent parts, one for each index of `groups`. The reference program is written for one: setup_inputs(seed, part) draws one part's arguments, and reference() takes and returns one part's arrays. A program takes and returns all parts, laid end to end along the dimension named above; each array names one. Nothing has to cross between parts.
Inputs may be any that keep to these rules, and one draw needn't show every extreme that they name: `near_lists`: entry 0 of every list is 4, the leaf itself; code k names the leaf k // 3 - 1 rows and k % 3 - 1 columns away, and repeats may occur. `filament_leaf`: leaves are numbered row by row over 8 x 32. Device d along gx+gy+gz holds the 2 x 8 leaves of leaf rows (d // (2 * 2)) * 2 on and leaf columns (d % (2 * 2)) * 8 on. Of the 512 filaments of one device, at most 64 lie over the leaves of any one device, and in every device's block some device gets exactly 64.
All inputs are finite; a program needn't handle non-finite values.
Results may differ from the reference program's by a relative error of at most 0.0049.
Values may be sent and summed in bfloat16 or wider, within the bound.
A program may use at most 128 MiB of HBM per device.

```python
import math
import jax
import jax.numpy as jnp
from jax import lax

P_SIZE = 128
FIL_DEV = 512
LEAF_R = 8
LEAF_C = 16
NEAR = 8
NX = 64
NY = 512
NXL = 8
NYL = 32
LC = 128
LEAF_ROWS_DEV = 2
LEAF_COLS_DEV = 8
LEAF_DEV = 16
OWNERS = 16
CAP = 64
FIL = 8192


def draw_inductance(key, part):
    spread_scale = 1.0 / math.sqrt(NEAR * LC)
    tile_shape = (NXL, NYL, NEAR, 2, LC, LC)
    entries = jnp.clip(jax.random.normal(key, tile_shape, jnp.float32), -6.0, 6.0)
    offdiag = jnp.clip(entries * spread_scale, -0.25, 0.25)
    selfmask = (jnp.arange(NEAR) == 0).astype(jnp.float32)[:, None, None, None]
    diagonal = selfmask * jnp.eye(LC, dtype=jnp.float32)[None, None, :, :]
    return (offdiag + diagonal).astype(jnp.bfloat16)


def draw_near_lists(key, part):
    codes = jax.random.randint(key, (NXL, NYL, NEAR), 0, 9, dtype=jnp.int32)
    return codes.at[:, :, 0].set(4)


def draw_filament_leaf(key, part):
    hot_key, block_key = jax.random.split(jax.random.fold_in(key, 7))
    ranked = jax.random.permutation(hot_key, OWNERS)
    heated = (ranked < OWNERS // 4).astype(jnp.int32)
    slot_total = OWNERS * CAP
    candidate = jnp.arange(slot_total, dtype=jnp.int32)
    owner_table = candidate // CAP
    owner_cols = NYL // LEAF_COLS_DEV

    def one_block(number):
        block_seed = jax.random.fold_in(block_key, number)
        jitter_key, pinned_key, leaf_key = jax.random.split(block_seed, 3)
        jitter = jax.random.randint(jitter_key, (slot_total,), 0, 1024, dtype=jnp.int32)
        pinned = jax.random.randint(pinned_key, (), 0, OWNERS, dtype=jnp.int32)
        priority = jitter + 512 * heated[owner_table] + 4096 * (owner_table == pinned).astype(jnp.int32)
        distinct = priority * slot_total + candidate
        ordered_values, chosen = lax.top_k(distinct, FIL_DEV)
        owner_ids = owner_table[chosen]
        local_ids = jax.random.randint(leaf_key, (FIL_DEV,), 0, LEAF_DEV, dtype=jnp.int32)
        leaf_row = owner_ids // owner_cols * LEAF_ROWS_DEV + local_ids // LEAF_COLS_DEV
        leaf_col = owner_ids % owner_cols * LEAF_COLS_DEV + local_ids % LEAF_COLS_DEV
        return leaf_row * NYL + leaf_col
    return lax.map(one_block, jnp.arange(OWNERS, dtype=jnp.int32)).reshape(-1).astype(jnp.int32)


def shard_levels(stream_key, shape, cuts, least, top_value):
    def one(axis_at, parts):
        heights = jax.random.uniform(jax.random.fold_in(jax.random.fold_in(stream_key, 6), axis_at), (parts,), jnp.float32, least / len(cuts), top_value / len(cuts))
        return jnp.repeat(jnp.exp(heights), shape[axis_at] // parts).reshape((-1,) + (1,) * (len(shape) - axis_at - 1))

    loudness = one(*cuts[0])
    for cut in cuts[1:]:
        loudness = loudness * one(*cut)
    return loudness


def centred(rng, shape, width, most, cuts=(), kind=jnp.bfloat16):
    level = shard_levels(rng, shape, cuts, -0.22, 0.18) if cuts else 1.0
    array = jax.random.normal(rng, shape, jnp.float32) * width * level
    return jnp.minimum(jnp.maximum(array, -most), most).astype(kind)


def setup_inputs(seed: int = 0, part: int = 0) -> dict:
    key_of = jax.random.split(jax.random.key(seed), 7)
    part_splits = jax.random.split(jax.random.fold_in(key_of[6], part), 7)
    stream = centred(part_splits[0], (P_SIZE, NX, NY), 1.0, 6.0, ((1, 4), (2, 2)), jnp.float32)
    inductance = draw_inductance(jax.random.fold_in(jax.random.fold_in(key_of[6], part), 71), part)
    near_lists = draw_near_lists(jax.random.fold_in(jax.random.fold_in(key_of[6], part), 71), part)
    filament_leaf = draw_filament_leaf(jax.random.fold_in(jax.random.fold_in(key_of[6], part), 71), part)
    filament_current = centred(part_splits[4], (FIL, P_SIZE), 1.0, 6.0, ((0, 16),))
    filament_coupling = centred(part_splits[5], (FIL, 2, LC), 0.125, 0.75, ((0, 16),))
    return dict(stream=stream, inductance=inductance, near_lists=near_lists, filament_leaf=filament_leaf, filament_current=filament_current, filament_coupling=filament_coupling)


def plane_curl(padded):
    along_y = padded[:, 1:-1, 2:] - padded[:, 1:-1, :-2]
    along_x = padded[:, :-2, 1:-1] - padded[:, 2:, 1:-1]
    return jnp.stack([along_y, along_x])


def to_leaves(grid_values):
    components, port_count, row_count, col_count = grid_values.shape
    blocks = grid_values.reshape(components, port_count, row_count // LEAF_R, LEAF_R, col_count // LEAF_C, LEAF_C)
    blocks = blocks.transpose(2, 4, 0, 1, 3, 5)
    return blocks.reshape(row_count // LEAF_R, col_count // LEAF_C, components, port_count, LEAF_R * LEAF_C)


def from_leaves(leaves):
    leaf_rows, leaf_cols, components, port_count, leaf_cells = leaves.shape
    blocks = leaves.reshape(leaf_rows, leaf_cols, components, port_count, LEAF_R, LEAF_C)
    blocks = blocks.transpose(2, 3, 0, 4, 1, 5)
    return blocks.reshape(components, port_count, leaf_rows * LEAF_R, leaf_cols * LEAF_C)


def reference(stream, inductance, near_lists, filament_leaf, filament_current, filament_coupling):
    padded = jnp.pad(stream, ((0, 0), (1, 1), (1, 1)))
    currents = plane_curl(padded).astype(jnp.bfloat16)
    leaves = to_leaves(currents)
    bordered = jnp.pad(leaves, ((1, 1), (1, 1), (0, 0), (0, 0), (0, 0)))
    row_stride = NYL + 2
    flattened = bordered.reshape((NXL + 2) * row_stride, 2, P_SIZE, LC)
    row_shift = near_lists // 3 - 1
    col_shift = near_lists % 3 - 1
    source = (jnp.arange(NXL, dtype=jnp.int32)[:, None, None] + 1 + row_shift) * row_stride
    source = (source + jnp.arange(NYL, dtype=jnp.int32)[None, :, None] + 1 + col_shift).astype(jnp.int32)

    def one_row(operands):
        kernels, chosen = operands
        gathered = jnp.take(flattened, chosen.reshape(-1), axis=0).reshape(NYL, NEAR, 2, P_SIZE, LC)
        return jnp.einsum("jncab,jncpb->jcpa", kernels.astype(jnp.float32), gathered.astype(jnp.float32))

    near_field = lax.map(one_row, (inductance, source))

    leaf_total = NXL * NYL
    leaves_flat = leaves.reshape(leaf_total, 2, P_SIZE, LC)

    def one_block(carried, operands):
        leaf_ids, current, coupling = operands
        current_wide = current.astype(jnp.float32)
        coupling_wide = coupling.astype(jnp.float32)
        beneath = jnp.take(leaves_flat, leaf_ids, axis=0).astype(jnp.float32)
        voltage = jnp.einsum("fca,fcpa->fp", coupling_wide, beneath)
        deposit = jnp.einsum("fca,fp->fcpa", coupling_wide, current_wide)
        carried = carried.at[leaf_ids].add(deposit)
        return carried, voltage.astype(jnp.bfloat16)

    initial = jnp.zeros((leaf_total, 2, P_SIZE, LC), jnp.float32)
    filament_field, voltages = lax.scan(
        one_block,
        initial,
        (filament_leaf.reshape(OWNERS, FIL_DEV).astype(jnp.int32),
         filament_current.reshape(OWNERS, FIL_DEV, P_SIZE),
         filament_coupling.reshape(OWNERS, FIL_DEV, 2, LC)))
    total_field = (near_field + filament_field.reshape(NXL, NYL, 2, P_SIZE, LC)).astype(jnp.bfloat16)
    grid_field = jnp.pad(from_leaves(total_field), ((0, 0), (0, 0), (1, 1), (1, 1))).astype(jnp.float32)
    x_field = grid_field[0]
    y_field = grid_field[1]
    loop_voltage = (x_field[:, 1:-1, :-2] - x_field[:, 1:-1, 2:]) + (y_field[:, 2:, 1:-1] - y_field[:, :-2, 1:-1])
    return loop_voltage, voltages.reshape(FIL, P_SIZE)
```

```python
import functools

import jax
import jax.numpy as jnp
from jax import lax
from jax.experimental import pallas as pl
from jax.experimental.pallas import tpu as pltpu
from jax.sharding import PartitionSpec as P

LEAF_R = 8
LEAF_C = 16
LANES = 128
BF = jnp.bfloat16
F32 = jnp.float32


def edges(value, axes, dim):
    size, length = lax.axis_size(axes), value.shape[dim]
    up = [(i, i + 1) for i in range(size - 1)]
    down = [(j, i) for i, j in up]
    last = lax.index_in_dim(value, length - 1, axis=dim, keepdims=False)
    first = lax.index_in_dim(value, 0, axis=dim, keepdims=False)
    before = lax.ppermute(last, axes, up)
    after = lax.ppermute(first, axes, down)
    return jnp.expand_dims(before, dim), jnp.expand_dims(after, dim)


def to_leaves(grid_values):
    components, port_count, row_count, col_count = grid_values.shape
    blocks = grid_values.reshape(
        components, port_count, row_count // LEAF_R, LEAF_R, col_count // LEAF_C, LEAF_C
    )
    blocks = blocks.transpose(2, 4, 0, 1, 3, 5)
    return blocks.reshape(
        row_count // LEAF_R, col_count // LEAF_C, components, port_count, LEAF_R * LEAF_C
    )


def from_leaves(leaves):
    leaf_rows, leaf_cols, components, port_count, leaf_cells = leaves.shape
    blocks = leaves.reshape(leaf_rows, leaf_cols, components, port_count, LEAF_R, LEAF_C)
    blocks = blocks.transpose(2, 3, 0, 4, 1, 5)
    return blocks.reshape(components, port_count, leaf_rows * LEAF_R, leaf_cols * LEAF_C)


def kernel(
    dims, near_ref, leaves_ref, send_ref, ids_ref, ind_hbm, field_ref, ret_ref,
    bordered, got, got_ids, ind, near_acc, volt, ret_send, current_t,
    ind_sem, halo_send, halo_recv, block_send, block_recv, id_send, id_recv, ret_ssem, ret_rsem,
):
    nx, ny, nz = dims
    nyz = ny * nz
    owners = nx * nyz
    leaf_rows, leaf_cols = leaves_ref.shape[:2]
    near_count = ind.shape[1]
    cap = send_ref.shape[1]
    slots = owners * cap
    mx, my, mz = lax.axis_index("gx"), lax.axis_index("gy"), lax.axis_index("gz")
    mc = my * nz + mz
    me = mx * nyz + mc

    def device(x, c):
        return {"gx": x, "gy": c // nz, "gz": c % nz}

    def peer(d):
        return device(d // nyz, d % nyz)

    ind_copy = pltpu.make_async_copy(ind_hbm, ind, ind_sem)
    ind_copy.start()
    barrier = pltpu.get_barrier_semaphore()

    @pl.loop(1, owners)
    def _(k):
        pl.semaphore_signal(
            barrier, inc=1, device_id=peer((me + k) % owners), device_id_type=pl.DeviceIdType.MESH
        )

    for r in range(leaf_rows):
        for j in range(leaf_cols):
            bordered[r + 1, j + 1] = leaves_ref[r, j]

    near_mesh = pl.DeviceIdType.MESH
    row_in = pl.ds(0, leaf_rows)
    row_at = pl.ds(1, leaf_rows)
    col_in = pl.ds(0, leaf_cols)
    col_at = pl.ds(1, leaf_cols)
    one = pl.ds(0, 1)
    plans = []
    for dx in (-1, 0, 1):
        for dc in (-1, 0, 1):
            if dx == 0 and dc == 0:
                continue
            src_r = row_in if dx == 0 else pl.ds(0 if dx < 0 else leaf_rows - 1, 1)
            dst_r = row_at if dx == 0 else pl.ds(leaf_rows + 1 if dx < 0 else 0, 1)
            src_c = col_in if dc == 0 else pl.ds(0 if dc < 0 else leaf_cols - 1, 1)
            dst_c = col_at if dc == 0 else pl.ds(leaf_cols + 1 if dc < 0 else 0, 1)
            plans.append((dx, dc, src_r, src_c, dst_r, dst_c))

    def halo(number):
        dx, dc, src_r, src_c, dst_r, dst_c = plans[number]
        return pltpu.make_async_remote_copy(
            src_ref=leaves_ref.at[src_r, src_c],
            dst_ref=bordered.at[dst_r, dst_c],
            send_sem=halo_send.at[number],
            recv_sem=halo_recv.at[number],
            device_id=device(mx + dx, mc + dc),
            device_id_type=near_mesh,
        )

    def inside(dx, dc):
        x, c = mx + dx, mc + dc
        return (x >= 0) & (x < nx) & (c >= 0) & (c < nyz)

    for number, (dx, dc, _, _, dst_r, dst_c) in enumerate(plans):
        @pl.when(jnp.logical_not(inside(-dx, -dc)))
        def _():
            view = bordered.at[dst_r, dst_c]
            view[...] = jnp.zeros(view.shape, BF)

    pl.semaphore_wait(barrier, owners - 1)

    for number, (dx, dc, _, _, _, _) in enumerate(plans):
        @pl.when(inside(dx, dc))
        def _():
            halo(number).start()

    def exchange(src, dst, ssem, rsem, d, slot):
        return pltpu.make_async_remote_copy(
            src_ref=src.at[d], dst_ref=dst.at[slot], send_sem=ssem.at[d], recv_sem=rsem.at[slot],
            device_id=peer(d), device_id_type=near_mesh,
        )

    @pl.loop(1, owners)
    def _(k):
        d = (me + k) % owners
        exchange(ids_ref, got_ids, id_send, id_recv, d, me).start()
        exchange(send_ref, got, block_send, block_recv, d, me).start()

    got[me] = send_ref[me]
    got_ids[me] = ids_ref[me]

    for number, (dx, dc, _, _, _, _) in enumerate(plans):
        @pl.when(inside(-dx, -dc))
        def _():
            halo(number).wait_recv()

    ind_copy.wait()

    @pl.loop(0, leaf_rows * leaf_cols)
    def _(l):
        for c in range(2):
            sources = jnp.concatenate(
                [bordered[near_ref[0, l * near_count + n], near_ref[1, l * near_count + n], c]
                 for n in range(near_count)], axis=1)
            tiles = jnp.concatenate([ind[l, n, c] for n in range(near_count)], axis=1)
            near_acc[l, :, c * LANES:(c + 1) * LANES] = lax.dot_general(
                sources, tiles, (((1,), (1,)), ((), ())), preferred_element_type=F32)

    @pl.loop(1, owners)
    def _(k):
        s = (me + k) % owners
        exchange(ids_ref, got_ids, id_send, id_recv, s, s).wait_recv()
        exchange(send_ref, got, block_send, block_recv, s, s).wait_recv()

    per_row = LANES // cap
    rows = []
    for g in range(slots // LANES):
        total = got_ids[g * per_row]
        for o in range(1, per_row):
            total = total + got_ids[g * per_row + o]
        rows.append(total)
    ids_row = jnp.concatenate(rows, axis=1) - 1.0
    coupling = got[:, :, : 2 * LANES].reshape(slots, 2 * LANES)
    current_t[...] = got[:, :, 2 * LANES:].reshape(slots, LANES).astype(F32).T.astype(BF)
    volt[...] = jnp.zeros_like(volt)

    @pl.loop(0, leaf_rows * leaf_cols)
    def _(l):
        hit = ids_row == l.astype(F32)
        plane = jnp.concatenate(
            [leaves_ref[l // leaf_cols, l % leaf_cols, c] for c in range(2)], axis=1)
        part = lax.dot_general(
            plane, coupling, (((1,), (1,)), ((), ())), preferred_element_type=F32)
        volt[...] += jnp.where(hit, part, 0.0)

    ret_send[...] = volt[...].T.astype(BF).reshape(owners, cap, LANES)

    @pl.loop(1, owners)
    def _(k):
        d = (me + k) % owners
        exchange(ret_send, ret_ref, ret_ssem, ret_rsem, d, me).start()

    ret_ref[me] = ret_send[me]

    @pl.loop(0, leaf_rows * leaf_cols)
    def _(l):
        hit = ids_row == l.astype(F32)
        masked = jnp.where(hit, current_t[...], jnp.zeros((), BF))
        part = near_acc[l] + jnp.dot(masked, coupling, preferred_element_type=F32)
        for c in range(2):
            field_ref[l, c] = part[:, c * LANES:(c + 1) * LANES].astype(BF)

    @pl.loop(1, owners)
    def _(k):
        s = (me + k) % owners
        exchange(ids_ref, got_ids, id_send, id_recv, s, s).wait_send()
        exchange(send_ref, got, block_send, block_recv, s, s).wait_send()
        exchange(ret_send, ret_ref, ret_ssem, ret_rsem, s, s).wait()

    for number, (dx, dc, _, _, _, _) in enumerate(plans):
        @pl.when(inside(dx, dc))
        def _():
            halo(number).wait_send()


def body(stream, inductance, near_lists, filament_leaf, filament_current, filament_coupling):
    port_count = stream.shape[0]
    leaf_rows, leaf_cols, near_count, _, leaf_cells, _ = inductance.shape
    leaf_count = leaf_rows * leaf_cols
    half_cols = leaf_cols * LEAF_C
    nx, ny, nz = lax.axis_size("gx"), lax.axis_size("gy"), lax.axis_size("gz")
    owners = nx * ny * nz
    first_col = lax.axis_index("gz") * half_cols
    me = (lax.axis_index("gx") * ny + lax.axis_index("gy")) * nz + lax.axis_index("gz")

    left, right = edges(stream, "gy", 2)
    above, below = edges(stream, "gx", 1)
    wide = jnp.concatenate([left, stream, right], axis=2)
    window = lax.dynamic_slice_in_dim(wide, first_col, half_cols + 2, 2)
    tall = lax.dynamic_slice_in_dim(
        jnp.concatenate([above, stream, below], axis=1), first_col, half_cols, 2)
    currents = jnp.stack([window[:, :, 2:] - window[:, :, :-2], tall[:, :-2] - tall[:, 2:]]).astype(BF)
    leaves = to_leaves(currents)

    row_index = jnp.arange(leaf_rows, dtype=jnp.int32)[:, None, None] + near_lists // 3
    col_index = jnp.arange(leaf_cols, dtype=jnp.int32)[None, :, None] + near_lists % 3
    near_index = jnp.stack([row_index.reshape(-1), col_index.reshape(-1)])

    filament_count = filament_leaf.shape[0]
    capacity = max(16, 2 * filament_count // owners)
    slot_count = owners * capacity
    plane_cols = leaf_cols * ny * nz
    leaf_row = filament_leaf // plane_cols
    leaf_col = filament_leaf % plane_cols
    owner_ids = leaf_row // leaf_rows * (ny * nz) + leaf_col // leaf_cols
    local_ids = leaf_row % leaf_rows * leaf_cols + leaf_col % leaf_cols
    owner_hits = owner_ids[:, None] == jnp.arange(owners, dtype=jnp.int32)[None, :]
    numbers = jnp.arange(filament_count, dtype=jnp.int32)
    earlier = (numbers[None, :] < numbers[:, None]).astype(BF)
    ranks = jnp.dot(earlier, owner_hits.astype(BF), preferred_element_type=F32)
    position = jnp.sum(jnp.where(owner_hits, ranks, 0.0), axis=1).astype(jnp.int32)
    target_slot = owner_ids * capacity + position
    placement_mask = target_slot[None, :] == jnp.arange(slot_count, dtype=jnp.int32)[:, None]
    placement = placement_mask.astype(BF)
    rows = jnp.concatenate(
        [filament_coupling.reshape(filament_count, 2 * leaf_cells), filament_current], axis=1)
    send = jnp.dot(placement, rows, preferred_element_type=F32).astype(BF)
    send = send.reshape(owners, capacity, 2 * leaf_cells + port_count)
    sent_leaf = jnp.max(jnp.where(placement_mask, local_ids[None, :] + 1, 0), axis=1).astype(F32)
    per_row = LANES // capacity
    lane_part = (jnp.arange(per_row, dtype=jnp.int32) == me % per_row).astype(F32)
    ids = (sent_leaf.reshape(owners, 1, capacity) * lane_part[None, :, None]).reshape(owners, 1, LANES)

    vmem = pl.BlockSpec(memory_space=pltpu.VMEM)
    dma = pltpu.SemaphoreType.DMA
    field, returned = pl.pallas_call(
        functools.partial(kernel, (nx, ny, nz)),
        out_shape=(
            jax.ShapeDtypeStruct((leaf_count, 2, port_count, leaf_cells), BF),
            jax.ShapeDtypeStruct((owners, capacity, port_count), BF),
        ),
        in_specs=[pl.BlockSpec(memory_space=pltpu.SMEM), vmem, vmem, vmem,
                  pl.BlockSpec(memory_space=pl.ANY)],
        out_specs=(vmem, vmem),
        scratch_shapes=[
            pltpu.VMEM((leaf_rows + 2, leaf_cols + 2, 2, port_count, leaf_cells), BF),
            pltpu.VMEM(send.shape, BF),
            pltpu.VMEM(ids.shape, F32),
            pltpu.VMEM((leaf_count, near_count, 2, leaf_cells, leaf_cells), BF),
            pltpu.VMEM((leaf_count, port_count, 2 * leaf_cells), F32),
            pltpu.VMEM((port_count, slot_count), F32),
            pltpu.VMEM((owners, capacity, port_count), BF),
            pltpu.VMEM((port_count, slot_count), BF),
            dma, dma((8,)), dma((8,)),
            dma((owners,)), dma((owners,)), dma((owners,)), dma((owners,)),
            dma((owners,)), dma((owners,)),
        ],
        compiler_params=pltpu.CompilerParams(
            collective_id=0, has_side_effects=True, vmem_limit_bytes=40 * 2**20),
        cost_estimate=pl.CostEstimate(
            flops=3 * 2 * 2**29, bytes_accessed=12 * 2**20, transcendentals=0),
    )(near_index, leaves, send, ids,
      inductance.reshape(leaf_count, near_count, 2, leaf_cells, leaf_cells))

    filament_voltage = lax.dot_general(
        placement, returned.reshape(slot_count, port_count), (((0,), (0,)), ((), ())),
        preferred_element_type=F32).astype(BF)
    grid_field = from_leaves(field.reshape(leaf_rows, leaf_cols, 2, port_count, leaf_cells))
    x_field, y_field = grid_field[0], grid_field[1]
    left, right = edges(x_field, ("gy", "gz"), 2)
    above, below = edges(y_field, "gx", 1)
    x_wide = jnp.concatenate([left, x_field, right], axis=2).astype(F32)
    y_tall = jnp.concatenate([above, y_field, below], axis=1).astype(F32)
    loop_voltage = (x_wide[:, :, :-2] - x_wide[:, :, 2:]) + (y_tall[:, 2:] - y_tall[:, :-2])
    return (loop_voltage, filament_voltage)


def solution(mesh):
    return jax.shard_map(
        body,
        mesh=mesh,
        in_specs=(
            P("groups", "gx", "gy"),
            P(("groups", "gx"), ("gy", "gz"), None, None, None, None),
            P(("groups", "gx"), ("gy", "gz"), None),
            P(("groups", "gx", "gy", "gz")),
            P(("groups", "gx", "gy", "gz"), None),
            P(("groups", "gx", "gy", "gz"), None, None),
        ),
        out_specs=(P("groups", "gx", ("gy", "gz")), P(("groups", "gx", "gy", "gz"), None)),
        check_vma=False,
    )
```

```python
import functools

import jax
import jax.numpy as jnp
from jax import lax
from jax.experimental import pallas as pl
from jax.experimental.pallas import tpu as pltpu
from jax.sharding import PartitionSpec as P

LEAF_R = 8
LEAF_C = 16
LANES = 128
BF = jnp.bfloat16
F32 = jnp.float32


def exchange_blocks(values):
    lane_block = lax.broadcasted_iota(jnp.int32, values[0].shape, 1) // LEAF_C
    values = list(values)
    for bit in (1, 2, 4):
        low = (lane_block & bit) == 0
        shift = bit * LEAF_C
        for r in range(LEAF_R):
            if r & bit:
                continue
            a, b = values[r], values[r | bit]
            values[r] = jnp.where(low, a, pltpu.roll(b, shift, 1))
            values[r | bit] = jnp.where(low, pltpu.roll(a, LANES - shift, 1), b)
    return values


def sides(mid, before, after):
    lane = lax.broadcasted_iota(jnp.int32, mid.shape, 1)
    left = jnp.where(lane == 0, before, pltpu.roll(mid, 1, 1))
    right = jnp.where(lane == LANES - 1, after, pltpu.roll(mid, LANES - 1, 1))
    return left, right


CHUNK = 32


def kernel(
    dims, near_ref, tile_ref, send_ref, ids_ref, ind_hbm, loop_ref, ret_ref,
    stream_ref, bordered, planes, got, got_ids, ind, acc, ret_send, grid,
    col_out, row_in, col_in, frow_out, fcol_out, frow_in, fcol_in,
    ind_sem, halo_send, halo_recv, edge_send, edge_recv, fedge_send, fedge_recv,
    block_send, block_recv, id_send, id_recv, ret_ssem, ret_rsem,
):
    nx, ny, nz = dims
    nyz = ny * nz
    owners = nx * nyz
    leaf_rows, leaf_cols = bordered.shape[0] - 2, bordered.shape[1] - 2
    leaf_count = leaf_rows * leaf_cols
    ports, row_count = tile_ref.shape[:2]
    near_count = ind.shape[1]
    cap = send_ref.shape[1]
    mx, my, mz = lax.axis_index("gx"), lax.axis_index("gy"), lax.axis_index("gz")
    mc = my * nz + mz
    me = mx * nyz + mc
    mesh_id = pl.DeviceIdType.MESH

    def device(x, c):
        return {"gx": x, "gy": c // nz, "gz": c % nz}

    def peer(d):
        return device(d // nyz, d % nyz)

    def inside(dx, dc):
        x, c = mx + dx, mc + dc
        return (x >= 0) & (x < nx) & (c >= 0) & (c < nyz)

    ind_copy = pltpu.make_async_copy(ind_hbm, ind, ind_sem)
    ind_copy.start()
    barrier = pltpu.get_barrier_semaphore()

    @pl.loop(1, owners)
    def _(k):
        pl.semaphore_signal(
            barrier, inc=1, device_id=peer((me + k) % owners), device_id_type=mesh_id)

    lane = lax.broadcasted_iota(jnp.int32, (CHUNK, LANES), 1)

    def chunk(q):
        return pl.ds(pl.multiple_of(q * CHUNK, CHUNK), CHUNK)

    def gather_columns(source, target):
        @pl.loop(0, ports // CHUNK)
        def _(q):
            for side, at in ((0, 0), (1, LANES - 1)):
                total = jnp.zeros((CHUNK, LANES), F32)
                for x in range(row_count):
                    total = jnp.where(lane == x, source[x, chunk(q)][:, at:at + 1], total)
                target[side, chunk(q)] = total.astype(target.dtype)

    steps = ((-1, 0, 0, 1), (1, 0, 1, 0), (0, -1, 0, 1), (0, 1, 1, 0))

    def edge(number, first_row, last_row, col_from, row_to, col_to, ssem, rsem):
        dx, dc, mine, theirs = steps[number]
        if dx:
            src, dst = (last_row if mine else first_row), row_to.at[theirs]
        else:
            src, dst = col_from.at[mine], col_to.at[theirs]
        return pltpu.make_async_remote_copy(
            src_ref=src, dst_ref=dst, send_sem=ssem.at[number], recv_sem=rsem.at[number],
            device_id=device(mx + dx, mc + dc), device_id_type=mesh_id)

    def stream_edge(number):
        return edge(number, stream_ref.at[0], stream_ref.at[row_count - 1], col_out, row_in, col_in,
                    edge_send, edge_recv)

    def field_edge(number):
        return edge(number, frow_out.at[0], frow_out.at[1], fcol_out, frow_in, fcol_in,
                    fedge_send, fedge_recv)

    all_rows, inner_cols = pl.ds(0, leaf_rows + 2), pl.ds(1, leaf_cols)
    plans = (
        (-1, 0, pl.ds(1, 1), inner_cols, pl.ds(leaf_rows + 1, 1), inner_cols),
        (1, 0, pl.ds(leaf_rows, 1), inner_cols, pl.ds(0, 1), inner_cols),
        (0, -1, all_rows, pl.ds(1, 1), all_rows, pl.ds(leaf_cols + 1, 1)),
        (0, 1, all_rows, pl.ds(leaf_cols, 1), all_rows, pl.ds(0, 1)),
    )

    def halo(number):
        dx, dc, src_r, src_c, dst_r, dst_c = plans[number]
        return pltpu.make_async_remote_copy(
            src_ref=bordered.at[src_r, src_c], dst_ref=bordered.at[dst_r, dst_c],
            send_sem=halo_send.at[number], recv_sem=halo_recv.at[number],
            device_id=device(mx + dx, mc + dc), device_id_type=mesh_id)

    def over(moves, test_sign, action, numbers=range(4)):
        for number in numbers:
            move = moves[number]

            @pl.when(inside(test_sign * move[0], test_sign * move[1]))
            def _():
                action(number)

    def exchange(src, dst, ssem, rsem, d, slot):
        return pltpu.make_async_remote_copy(
            src_ref=src.at[d], dst_ref=dst.at[slot], send_sem=ssem.at[d], recv_sem=rsem.at[slot],
            device_id=peer(d), device_id_type=mesh_id)

    own_cols = pl.ds(pl.multiple_of(mz * LANES, LANES), LANES)

    @pl.loop(0, ports // CHUNK)
    def _(q):
        for x in range(row_count):
            stream_ref[x, chunk(q)] = tile_ref[chunk(q), x, own_cols]

    gather_columns(stream_ref, col_out)
    for number, (dx, dc, _, theirs) in enumerate(steps):
        @pl.when(jnp.logical_not(inside(-dx, -dc)))
        def _():
            for target in ((row_in, frow_in) if dx else (col_in, fcol_in)):
                target[theirs] = jnp.zeros(target.shape[1:], target.dtype)
    for dx, dc, _, _, dst_r, dst_c in plans:
        @pl.when(jnp.logical_not(inside(-dx, -dc)))
        def _():
            view = bordered.at[dst_r, dst_c]
            view[...] = jnp.zeros(view.shape, BF)

    pl.semaphore_wait(barrier, owners - 1)

    over(steps, 1, lambda number: stream_edge(number).start())

    def send_blocks(k):
        to = (mx + nx - k) % nx * nyz

        @pl.loop(1 if isinstance(k, int) and k == 0 else 0, nyz)
        def _(i):
            d = to + (mc + i) % nyz
            exchange(ids_ref, got_ids, id_send, id_recv, d, me).start()
            exchange(send_ref, got, block_send, block_recv, d, me).start()

    send_blocks(0)
    if nx > 1:
        send_blocks(1)

    got[me] = send_ref[me]
    got_ids[me] = ids_ref[me]

    over(steps, -1, lambda number: stream_edge(number).wait_recv())

    for lr in range(leaf_rows):
        @pl.loop(0, ports // CHUNK)
        def _(q):
            def row(x):
                if x < 0:
                    return row_in[0, chunk(q)]
                if x >= row_count:
                    return row_in[1, chunk(q)]
                return stream_ref[x, chunk(q)]

            before, after = col_in[0, chunk(q)], col_in[1, chunk(q)]
            along_y, along_x = [], []
            for x in range(lr * LEAF_R, (lr + 1) * LEAF_R):
                left, right = sides(row(x), before[:, x:x + 1], after[:, x:x + 1])
                along_y.append(right - left)
                along_x.append(row(x - 1) - row(x + 1))
            for c, values in enumerate((along_y, along_x)):
                for j, value in enumerate(exchange_blocks(values)):
                    rounded = value.astype(BF)
                    bordered[lr + 1, j + 1, c, chunk(q)] = rounded
                    at = pl.multiple_of((lr * leaf_cols + j) * ports + q * CHUNK, CHUNK)
                    planes[pl.ds(at, CHUNK), c * LANES:(c + 1) * LANES] = rounded

    over(plans, 1, lambda number: halo(number).start(), (0, 1))

    @pl.loop(2, nx)
    def _(k):
        send_blocks(k)

    per_row = LANES // cap
    width = nyz * cap
    stack = 4
    tall = stack * ports

    def work_on_blocks(k):
        first = isinstance(k, int) and k == 0
        base = (mx + k) % nx * nyz

        @pl.loop(1 if first else 0, nyz)
        def _(i):
            s = base + (mc + i) % nyz
            exchange(ids_ref, got_ids, id_send, id_recv, s, s).wait_recv()
            exchange(send_ref, got, block_send, block_recv, s, s).wait_recv()

        rows = []
        for g in range(nyz // per_row):
            total = got_ids[base + g * per_row]
            for o in range(1, per_row):
                total = total + got_ids[base + g * per_row + o]
            rows.append(total)
        ids_row = jnp.concatenate(rows, axis=1) - 1.0
        block = got[pl.ds(base, nyz)]
        coupling = block[:, :, : 2 * LANES].reshape(width, 2 * LANES)
        current_t = block[:, :, 2 * LANES:].reshape(width, LANES).astype(F32).T.astype(BF)

        volt = jnp.zeros((ports, width), F32)
        for b in range(leaf_count // stack):
            part = lax.dot_general(
                planes[b * tall:(b + 1) * tall, :], coupling, (((1,), (1,)), ((), ())),
                preferred_element_type=F32)
            for i in range(stack):
                hit = ids_row == float(b * stack + i)
                volt = volt + jnp.where(hit, part[i * ports:(i + 1) * ports], 0.0)
        ret_send[pl.ds(base, nyz)] = volt.T.astype(BF).reshape(nyz, cap, LANES)

        @pl.loop(1 if first else 0, nyz)
        def _(i):
            d = base + (mc + i) % nyz
            exchange(ret_send, ret_ref, ret_ssem, ret_rsem, d, me).start()

        for b in range(leaf_count // stack):
            masked = jnp.concatenate(
                [jnp.where(ids_row == float(b * stack + i), current_t, jnp.zeros((), BF))
                 for i in range(stack)], axis=0)
            part = jnp.dot(masked, coupling, preferred_element_type=F32)
            if first:
                acc[b * tall:(b + 1) * tall, :] = part
            else:
                acc[b * tall:(b + 1) * tall, :] += part

    work_on_blocks(0)
    ret_ref[me] = ret_send[me]
    over(plans, -1, lambda number: halo(number).wait_recv(), (0, 1))
    over(plans, 1, lambda number: halo(number).start(), (2, 3))
    if nx > 1:
        work_on_blocks(1)

    over(plans, -1, lambda number: halo(number).wait_recv(), (2, 3))
    ind_copy.wait()

    @pl.loop(0, leaf_count)
    def _(l):
        r, j = l // leaf_cols, l % leaf_cols
        codes = [near_ref[r, j, n] for n in range(near_count)]
        at = pl.ds(pl.multiple_of(l * ports, ports), ports)
        for c in range(2):
            sources = jnp.concatenate(
                [bordered[r + code // 3, j + code % 3, c] for code in codes], axis=1)
            tiles = jnp.concatenate([ind[l, n, c] for n in range(near_count)], axis=1)
            acc[at, c * LANES:(c + 1) * LANES] += lax.dot_general(
                sources, tiles, (((1,), (1,)), ((), ())), preferred_element_type=F32)

    @pl.loop(2, nx)
    def _(k):
        work_on_blocks(k)

    for lr in range(leaf_rows):
        for c in range(2):
            @pl.loop(0, ports // CHUNK)
            def _(q):
                values = []
                for j in range(leaf_cols):
                    at = pl.multiple_of((lr * leaf_cols + j) * ports + q * CHUNK, CHUNK)
                    value = acc[pl.ds(at, CHUNK), c * LANES:(c + 1) * LANES]
                    values.append(value.astype(BF).astype(F32))
                for r, value in enumerate(exchange_blocks(values)):
                    grid[c, lr * LEAF_R + r, chunk(q)] = value

    frow_out[0] = grid[1, 0].astype(BF)
    frow_out[1] = grid[1, row_count - 1].astype(BF)
    gather_columns(grid.at[0], fcol_out)
    over(steps, 1, lambda number: field_edge(number).start())
    over(steps, -1, lambda number: field_edge(number).wait_recv())

    @pl.loop(0, ports // CHUNK)
    def _(q):
        def row(x):
            if x < 0:
                return frow_in[0, chunk(q)].astype(F32)
            if x >= row_count:
                return frow_in[1, chunk(q)].astype(F32)
            return grid[1, x, chunk(q)]

        before, after = fcol_in[0, chunk(q)].astype(F32), fcol_in[1, chunk(q)].astype(F32)
        for x in range(row_count):
            left, right = sides(grid[0, x, chunk(q)], before[:, x:x + 1], after[:, x:x + 1])
            loop_ref[chunk(q), x, :] = (left - right) + (row(x + 1) - row(x - 1))

    @pl.loop(1, owners)
    def _(k):
        s = (me + k) % owners
        exchange(ids_ref, got_ids, id_send, id_recv, s, s).wait_send()
        exchange(send_ref, got, block_send, block_recv, s, s).wait_send()
        exchange(ret_send, ret_ref, ret_ssem, ret_rsem, s, s).wait()

    over(steps, 1, lambda number: stream_edge(number).wait_send())
    over(steps, 1, lambda number: field_edge(number).wait_send())
    over(plans, 1, lambda number: halo(number).wait_send())


def body(stream, inductance, near_lists, filament_leaf, filament_current, filament_coupling):
    port_count = stream.shape[0]
    leaf_rows, leaf_cols, near_count, _, leaf_cells, _ = inductance.shape
    leaf_count = leaf_rows * leaf_cols
    nx, ny, nz = lax.axis_size("gx"), lax.axis_size("gy"), lax.axis_size("gz")
    owners = nx * ny * nz
    me = (lax.axis_index("gx") * ny + lax.axis_index("gy")) * nz + lax.axis_index("gz")

    row_count = stream.shape[1]
    filament_count = filament_leaf.shape[0]
    capacity = max(16, 2 * filament_count // owners)
    slot_count = owners * capacity
    plane_cols = leaf_cols * ny * nz
    leaf_row = filament_leaf // plane_cols
    leaf_col = filament_leaf % plane_cols
    owner_ids = leaf_row // leaf_rows * (ny * nz) + leaf_col // leaf_cols
    local_ids = leaf_row % leaf_rows * leaf_cols + leaf_col % leaf_cols
    owner_hits = owner_ids[:, None] == jnp.arange(owners, dtype=jnp.int32)[None, :]
    numbers = jnp.arange(filament_count, dtype=jnp.int32)
    earlier = (numbers[None, :] < numbers[:, None]).astype(BF)
    ranks = jnp.dot(earlier, owner_hits.astype(BF), preferred_element_type=F32)
    position = jnp.sum(jnp.where(owner_hits, ranks, 0.0), axis=1).astype(jnp.int32)
    target_slot = owner_ids * capacity + position
    placement_mask = target_slot[None, :] == jnp.arange(slot_count, dtype=jnp.int32)[:, None]
    placement = placement_mask.astype(BF)
    rows = jnp.concatenate(
        [filament_coupling.reshape(filament_count, 2 * leaf_cells), filament_current], axis=1)
    send = jnp.dot(placement, rows, preferred_element_type=F32).astype(BF)
    send = send.reshape(owners, capacity, 2 * leaf_cells + port_count)
    sent_leaf = jnp.max(jnp.where(placement_mask, local_ids[None, :] + 1, 0), axis=1).astype(F32)
    per_row = LANES // capacity
    lane_part = (jnp.arange(per_row, dtype=jnp.int32) == me % per_row).astype(F32)
    ids = (sent_leaf.reshape(owners, 1, capacity) * lane_part[None, :, None]).reshape(owners, 1, LANES)

    vmem = pl.BlockSpec(memory_space=pltpu.VMEM)
    dma = pltpu.SemaphoreType.DMA
    tile = (port_count, LANES)
    loop_voltage, returned = pl.pallas_call(
        functools.partial(kernel, (nx, ny, nz)),
        out_shape=(
            jax.ShapeDtypeStruct((port_count, row_count, LANES), F32),
            jax.ShapeDtypeStruct((owners, capacity, port_count), BF),
        ),
        in_specs=[pl.BlockSpec(memory_space=pltpu.SMEM), vmem, vmem, vmem,
                  pl.BlockSpec(memory_space=pl.ANY)],
        out_specs=(vmem, vmem),
        scratch_shapes=[
            pltpu.VMEM((row_count,) + tile, F32),
            pltpu.VMEM((leaf_rows + 2, leaf_cols + 2, 2, port_count, leaf_cells), BF),
            pltpu.VMEM((leaf_count * port_count, 2 * leaf_cells), BF),
            pltpu.VMEM(send.shape, BF),
            pltpu.VMEM(ids.shape, F32),
            pltpu.VMEM((leaf_count, near_count, 2, leaf_cells, leaf_cells), BF),
            pltpu.VMEM((leaf_count * port_count, 2 * leaf_cells), F32),
            pltpu.VMEM((owners, capacity, port_count), BF),
            pltpu.VMEM((2, row_count) + tile, F32),
            pltpu.VMEM((2,) + tile, F32), pltpu.VMEM((2,) + tile, F32), pltpu.VMEM((2,) + tile, F32),
            pltpu.VMEM((2,) + tile, BF), pltpu.VMEM((2,) + tile, BF),
            pltpu.VMEM((2,) + tile, BF), pltpu.VMEM((2,) + tile, BF),
            dma, dma((4,)), dma((4,)), dma((4,)), dma((4,)), dma((4,)), dma((4,)),
            dma((owners,)), dma((owners,)), dma((owners,)), dma((owners,)),
            dma((owners,)), dma((owners,)),
        ],
        compiler_params=pltpu.CompilerParams(
            collective_id=0, has_side_effects=True, vmem_limit_bytes=56 * 2**20),
        cost_estimate=pl.CostEstimate(
            flops=3 * 2 * 2**29, bytes_accessed=12 * 2**20, transcendentals=0),
    )(near_lists, stream, send, ids,
      inductance.reshape(leaf_count, near_count, 2, leaf_cells, leaf_cells))

    filament_voltage = lax.dot_general(
        placement, returned.reshape(slot_count, port_count), (((0,), (0,)), ((), ())),
        preferred_element_type=F32).astype(BF)
    return (loop_voltage, filament_voltage)


def solution(mesh):
    return jax.shard_map(
        body,
        mesh=mesh,
        in_specs=(
            P("groups", "gx", "gy"),
            P(("groups", "gx"), ("gy", "gz"), None, None, None, None),
            P(("groups", "gx"), ("gy", "gz"), None),
            P(("groups", "gx", "gy", "gz")),
            P(("groups", "gx", "gy", "gz"), None),
            P(("groups", "gx", "gy", "gz"), None, None),
        ),
        out_specs=(P("groups", "gx", ("gy", "gz")), P(("groups", "gx", "gy", "gz"), None)),
        check_vma=False,
    )
```

```python
import functools

import jax
import jax.numpy as jnp
from jax import lax
from jax.experimental import pallas as pl
from jax.experimental.pallas import tpu as pltpu
from jax.sharding import PartitionSpec as P

LEAF_R = 8
LEAF_C = 16
LANES = 128
BF = jnp.bfloat16
F32 = jnp.float32


def exchange_blocks(values):
    lane_block = lax.broadcasted_iota(jnp.int32, values[0].shape, 1) // LEAF_C
    values = list(values)
    for bit in (1, 2, 4):
        low = (lane_block & bit) == 0
        shift = bit * LEAF_C
        for r in range(LEAF_R):
            if r & bit:
                continue
            a, b = values[r], values[r | bit]
            values[r] = jnp.where(low, a, pltpu.roll(b, shift, 1))
            values[r | bit] = jnp.where(low, pltpu.roll(a, LANES - shift, 1), b)
    return values


def sides(mid, before, after):
    lane = lax.broadcasted_iota(jnp.int32, mid.shape, 1)
    left = jnp.where(lane == 0, before, pltpu.roll(mid, 1, 1))
    right = jnp.where(lane == LANES - 1, after, pltpu.roll(mid, LANES - 1, 1))
    return left, right


CHUNK = 32


def kernel(
    dims, near_ref, tile_ref, send_ref, ids_ref, ind_hbm, loop_ref, ret_ref,
    stream_ref, bordered, planes, got, got_ids, ind, acc, ret_send, grid,
    col_out, row_in, col_in, frow_out, fcol_out, frow_in, fcol_in,
    ind_sem, halo_send, halo_recv, edge_send, edge_recv, fedge_send, fedge_recv,
    block_send, block_recv, id_send, id_recv, ret_ssem, ret_rsem,
):
    nx, ny, nz = dims
    nyz = ny * nz
    owners = nx * nyz
    leaf_rows, leaf_cols = bordered.shape[0] - 2, bordered.shape[1] - 2
    leaf_count = leaf_rows * leaf_cols
    ports, row_count = tile_ref.shape[:2]
    near_count = ind.shape[1]
    cap = send_ref.shape[1]
    mx, my, mz = lax.axis_index("gx"), lax.axis_index("gy"), lax.axis_index("gz")
    mc = my * nz + mz
    me = mx * nyz + mc
    mesh_id = pl.DeviceIdType.MESH

    def device(x, c):
        return {"gx": x, "gy": c // nz, "gz": c % nz}

    def peer(d):
        return device(d // nyz, d % nyz)

    def inside(dx, dc):
        x, c = mx + dx, mc + dc
        return (x >= 0) & (x < nx) & (c >= 0) & (c < nyz)

    ind_copy = pltpu.make_async_copy(ind_hbm, ind, ind_sem)
    ind_copy.start()
    barrier = pltpu.get_barrier_semaphore()

    @pl.loop(1, owners)
    def _(k):
        pl.semaphore_signal(
            barrier, inc=1, device_id=peer((me + k) % owners), device_id_type=mesh_id)

    lane = lax.broadcasted_iota(jnp.int32, (CHUNK, LANES), 1)

    def chunk(q):
        return pl.ds(pl.multiple_of(q * CHUNK, CHUNK), CHUNK)

    def gather_columns(source, target):
        @pl.loop(0, ports // CHUNK)
        def _(q):
            for side, at in ((0, 0), (1, LANES - 1)):
                total = jnp.zeros((CHUNK, LANES), F32)
                for x in range(row_count):
                    total = jnp.where(lane == x, source[x, chunk(q)][:, at:at + 1], total)
                target[side, chunk(q)] = total.astype(target.dtype)

    steps = ((-1, 0, 0, 1), (1, 0, 1, 0), (0, -1, 0, 1), (0, 1, 1, 0))

    def edge(number, first_row, last_row, col_from, row_to, col_to, ssem, rsem):
        dx, dc, mine, theirs = steps[number]
        if dx:
            src, dst = (last_row if mine else first_row), row_to.at[theirs]
        else:
            src, dst = col_from.at[mine], col_to.at[theirs]
        return pltpu.make_async_remote_copy(
            src_ref=src, dst_ref=dst, send_sem=ssem.at[number], recv_sem=rsem.at[number],
            device_id=device(mx + dx, mc + dc), device_id_type=mesh_id)

    def stream_edge(number):
        return edge(number, stream_ref.at[0], stream_ref.at[row_count - 1], col_out, row_in, col_in,
                    edge_send, edge_recv)

    def field_edge(number):
        return edge(number, frow_out.at[0], frow_out.at[1], fcol_out, frow_in, fcol_in,
                    fedge_send, fedge_recv)

    every_r, every_c = pl.ds(1, leaf_rows), pl.ds(1, leaf_cols)
    plans = []
    for dx in (-1, 0, 1):
        for dc in (-1, 0, 1):
            if dx or dc:
                src_r = every_r if dx == 0 else pl.ds(1 if dx < 0 else leaf_rows, 1)
                dst_r = every_r if dx == 0 else pl.ds(leaf_rows + 1 if dx < 0 else 0, 1)
                src_c = every_c if dc == 0 else pl.ds(1 if dc < 0 else leaf_cols, 1)
                dst_c = every_c if dc == 0 else pl.ds(leaf_cols + 1 if dc < 0 else 0, 1)
                plans.append((dx, dc, src_r, src_c, dst_r, dst_c))

    def halo(number):
        dx, dc, src_r, src_c, dst_r, dst_c = plans[number]
        return pltpu.make_async_remote_copy(
            src_ref=bordered.at[src_r, src_c], dst_ref=bordered.at[dst_r, dst_c],
            send_sem=halo_send.at[number], recv_sem=halo_recv.at[number],
            device_id=device(mx + dx, mc + dc), device_id_type=mesh_id)

    def over(moves, test_sign, action):
        for number, move in enumerate(moves):
            @pl.when(inside(test_sign * move[0], test_sign * move[1]))
            def _():
                action(number)

    def exchange(src, dst, ssem, rsem, d, slot):
        return pltpu.make_async_remote_copy(
            src_ref=src.at[d], dst_ref=dst.at[slot], send_sem=ssem.at[d], recv_sem=rsem.at[slot],
            device_id=peer(d), device_id_type=mesh_id)

    own_cols = pl.ds(pl.multiple_of(mz * LANES, LANES), LANES)

    @pl.loop(0, ports // CHUNK)
    def _(q):
        for x in range(row_count):
            stream_ref[x, chunk(q)] = tile_ref[chunk(q), x, own_cols]

    gather_columns(stream_ref, col_out)
    for number, (dx, dc, _, theirs) in enumerate(steps):
        @pl.when(jnp.logical_not(inside(-dx, -dc)))
        def _():
            for target in ((row_in, frow_in) if dx else (col_in, fcol_in)):
                target[theirs] = jnp.zeros(target.shape[1:], target.dtype)
    for dx, dc, _, _, dst_r, dst_c in plans:
        @pl.when(jnp.logical_not(inside(-dx, -dc)))
        def _():
            view = bordered.at[dst_r, dst_c]
            view[...] = jnp.zeros(view.shape, BF)

    pl.semaphore_wait(barrier, owners - 1)

    over(steps, 1, lambda number: stream_edge(number).start())

    def send_blocks(k):
        to = (mx + nx - k) % nx * nyz

        @pl.loop(1 if isinstance(k, int) and k == 0 else 0, nyz)
        def _(i):
            d = to + (mc + i) % nyz
            exchange(ids_ref, got_ids, id_send, id_recv, d, me).start()
            exchange(send_ref, got, block_send, block_recv, d, me).start()

    far = nx // 2
    send_blocks(0)
    if far:
        send_blocks(far)

    got[me] = send_ref[me]
    got_ids[me] = ids_ref[me]

    over(steps, -1, lambda number: stream_edge(number).wait_recv())

    for lr in range(leaf_rows):
        @pl.loop(0, ports // CHUNK)
        def _(q):
            def row(x):
                if x < 0:
                    return row_in[0, chunk(q)]
                if x >= row_count:
                    return row_in[1, chunk(q)]
                return stream_ref[x, chunk(q)]

            before, after = col_in[0, chunk(q)], col_in[1, chunk(q)]
            along_y, along_x = [], []
            for x in range(lr * LEAF_R, (lr + 1) * LEAF_R):
                left, right = sides(row(x), before[:, x:x + 1], after[:, x:x + 1])
                along_y.append(right - left)
                along_x.append(row(x - 1) - row(x + 1))
            for c, values in enumerate((along_y, along_x)):
                for j, value in enumerate(exchange_blocks(values)):
                    rounded = value.astype(BF)
                    bordered[lr + 1, j + 1, c, chunk(q)] = rounded
                    at = pl.multiple_of((lr * leaf_cols + j) * ports + q * CHUNK, CHUNK)
                    planes[pl.ds(at, CHUNK), c * LANES:(c + 1) * LANES] = rounded

    over(plans, 1, lambda number: halo(number).start())

    def over_rest(action):
        pl.loop(1, far)(action)
        pl.loop(far + 1, nx)(action)

    over_rest(send_blocks)

    per_row = LANES // cap
    width = nyz * cap
    stack = 4
    tall = stack * ports

    def work_on_blocks(k):
        first = isinstance(k, int) and k == 0
        base = (mx + k) % nx * nyz

        @pl.loop(1 if first else 0, nyz)
        def _(i):
            s = base + (mc + i) % nyz
            exchange(ids_ref, got_ids, id_send, id_recv, s, s).wait_recv()
            exchange(send_ref, got, block_send, block_recv, s, s).wait_recv()

        rows = []
        for g in range(nyz // per_row):
            total = got_ids[base + g * per_row]
            for o in range(1, per_row):
                total = total + got_ids[base + g * per_row + o]
            rows.append(total)
        ids_row = jnp.concatenate(rows, axis=1) - 1.0
        block = got[pl.ds(base, nyz)]
        coupling = block[:, :, : 2 * LANES].reshape(width, 2 * LANES)
        current_t = block[:, :, 2 * LANES:].reshape(width, LANES).astype(F32).T.astype(BF)

        volt = jnp.zeros((ports, width), F32)
        for b in range(leaf_count // stack):
            part = lax.dot_general(
                planes[b * tall:(b + 1) * tall, :], coupling, (((1,), (1,)), ((), ())),
                preferred_element_type=F32)
            for i in range(stack):
                hit = ids_row == float(b * stack + i)
                volt = volt + jnp.where(hit, part[i * ports:(i + 1) * ports], 0.0)
        ret_send[pl.ds(base, nyz)] = volt.T.astype(BF).reshape(nyz, cap, LANES)

        @pl.loop(1 if first else 0, nyz)
        def _(i):
            d = base + (mc + i) % nyz
            exchange(ret_send, ret_ref, ret_ssem, ret_rsem, d, me).start()

        for b in range(leaf_count // stack):
            masked = jnp.concatenate(
                [jnp.where(ids_row == float(b * stack + i), current_t, jnp.zeros((), BF))
                 for i in range(stack)], axis=0)
            part = jnp.dot(masked, coupling, preferred_element_type=F32)
            if first:
                acc[b * tall:(b + 1) * tall, :] = part
            else:
                acc[b * tall:(b + 1) * tall, :] += part

    work_on_blocks(0)
    ret_ref[me] = ret_send[me]
    if far:
        work_on_blocks(far)

    over(plans, -1, lambda number: halo(number).wait_recv())
    ind_copy.wait()

    @pl.loop(0, leaf_count)
    def _(l):
        r, j = l // leaf_cols, l % leaf_cols
        codes = [near_ref[r, j, n] for n in range(near_count)]
        at = pl.ds(pl.multiple_of(l * ports, ports), ports)
        for c in range(2):
            sources = jnp.concatenate(
                [bordered[r + code // 3, j + code % 3, c] for code in codes], axis=1)
            tiles = jnp.concatenate([ind[l, n, c] for n in range(near_count)], axis=1)
            acc[at, c * LANES:(c + 1) * LANES] += lax.dot_general(
                sources, tiles, (((1,), (1,)), ((), ())), preferred_element_type=F32)

    over_rest(work_on_blocks)

    for lr in range(leaf_rows):
        for c in range(2):
            @pl.loop(0, ports // CHUNK)
            def _(q):
                values = []
                for j in range(leaf_cols):
                    at = pl.multiple_of((lr * leaf_cols + j) * ports + q * CHUNK, CHUNK)
                    value = acc[pl.ds(at, CHUNK), c * LANES:(c + 1) * LANES]
                    values.append(value.astype(BF).astype(F32))
                for r, value in enumerate(exchange_blocks(values)):
                    grid[c, lr * LEAF_R + r, chunk(q)] = value

    frow_out[0] = grid[1, 0].astype(BF)
    frow_out[1] = grid[1, row_count - 1].astype(BF)
    gather_columns(grid.at[0], fcol_out)
    over(steps, 1, lambda number: field_edge(number).start())
    over(steps, -1, lambda number: field_edge(number).wait_recv())

    @pl.loop(0, ports // CHUNK)
    def _(q):
        def row(x):
            if x < 0:
                return frow_in[0, chunk(q)].astype(F32)
            if x >= row_count:
                return frow_in[1, chunk(q)].astype(F32)
            return grid[1, x, chunk(q)]

        before, after = fcol_in[0, chunk(q)].astype(F32), fcol_in[1, chunk(q)].astype(F32)
        for x in range(row_count):
            left, right = sides(grid[0, x, chunk(q)], before[:, x:x + 1], after[:, x:x + 1])
            loop_ref[x, chunk(q)] = (left - right) + (row(x + 1) - row(x - 1))

    @pl.loop(1, owners)
    def _(k):
        s = (me + k) % owners
        exchange(ids_ref, got_ids, id_send, id_recv, s, s).wait_send()
        exchange(send_ref, got, block_send, block_recv, s, s).wait_send()
        exchange(ret_send, ret_ref, ret_ssem, ret_rsem, s, s).wait()

    over(steps, 1, lambda number: stream_edge(number).wait_send())
    over(steps, 1, lambda number: field_edge(number).wait_send())
    over(plans, 1, lambda number: halo(number).wait_send())


def body(stream, inductance, near_lists, filament_leaf, filament_current, filament_coupling):
    port_count = stream.shape[0]
    leaf_rows, leaf_cols, near_count, _, leaf_cells, _ = inductance.shape
    leaf_count = leaf_rows * leaf_cols
    nx, ny, nz = lax.axis_size("gx"), lax.axis_size("gy"), lax.axis_size("gz")
    owners = nx * ny * nz
    me = (lax.axis_index("gx") * ny + lax.axis_index("gy")) * nz + lax.axis_index("gz")

    row_count = stream.shape[1]
    filament_count = filament_leaf.shape[0]
    capacity = max(16, 2 * filament_count // owners)
    slot_count = owners * capacity
    plane_cols = leaf_cols * ny * nz
    leaf_row = filament_leaf // plane_cols
    leaf_col = filament_leaf % plane_cols
    owner_ids = leaf_row // leaf_rows * (ny * nz) + leaf_col // leaf_cols
    local_ids = leaf_row % leaf_rows * leaf_cols + leaf_col % leaf_cols
    owner_hits = owner_ids[:, None] == jnp.arange(owners, dtype=jnp.int32)[None, :]
    numbers = jnp.arange(filament_count, dtype=jnp.int32)
    earlier = (numbers[None, :] < numbers[:, None]).astype(BF)
    ranks = jnp.dot(earlier, owner_hits.astype(BF), preferred_element_type=F32)
    position = jnp.sum(jnp.where(owner_hits, ranks, 0.0), axis=1).astype(jnp.int32)
    target_slot = owner_ids * capacity + position
    placement_mask = target_slot[None, :] == jnp.arange(slot_count, dtype=jnp.int32)[:, None]
    placement = placement_mask.astype(BF)
    rows = jnp.concatenate(
        [filament_coupling.reshape(filament_count, 2 * leaf_cells), filament_current], axis=1)
    send = jnp.dot(placement, rows, preferred_element_type=F32).astype(BF)
    send = send.reshape(owners, capacity, 2 * leaf_cells + port_count)
    sent_leaf = jnp.max(jnp.where(placement_mask, local_ids[None, :] + 1, 0), axis=1).astype(F32)
    per_row = LANES // capacity
    lane_part = (jnp.arange(per_row, dtype=jnp.int32) == me % per_row).astype(F32)
    ids = (sent_leaf.reshape(owners, 1, capacity) * lane_part[None, :, None]).reshape(owners, 1, LANES)

    vmem = pl.BlockSpec(memory_space=pltpu.VMEM)
    dma = pltpu.SemaphoreType.DMA
    tile = (port_count, LANES)
    loop_rows, returned = pl.pallas_call(
        functools.partial(kernel, (nx, ny, nz)),
        out_shape=(
            jax.ShapeDtypeStruct((row_count,) + tile, F32),
            jax.ShapeDtypeStruct((owners, capacity, port_count), BF),
        ),
        in_specs=[pl.BlockSpec(memory_space=pltpu.SMEM), vmem, vmem, vmem,
                  pl.BlockSpec(memory_space=pl.ANY)],
        out_specs=(vmem, vmem),
        scratch_shapes=[
            pltpu.VMEM((row_count,) + tile, F32),
            pltpu.VMEM((leaf_rows + 2, leaf_cols + 2, 2, port_count, leaf_cells), BF),
            pltpu.VMEM((leaf_count * port_count, 2 * leaf_cells), BF),
            pltpu.VMEM(send.shape, BF),
            pltpu.VMEM(ids.shape, F32),
            pltpu.VMEM((leaf_count, near_count, 2, leaf_cells, leaf_cells), BF),
            pltpu.VMEM((leaf_count * port_count, 2 * leaf_cells), F32),
            pltpu.VMEM((owners, capacity, port_count), BF),
            pltpu.VMEM((2, row_count) + tile, F32),
            pltpu.VMEM((2,) + tile, F32), pltpu.VMEM((2,) + tile, F32), pltpu.VMEM((2,) + tile, F32),
            pltpu.VMEM((2,) + tile, BF), pltpu.VMEM((2,) + tile, BF),
            pltpu.VMEM((2,) + tile, BF), pltpu.VMEM((2,) + tile, BF),
            dma, dma((8,)), dma((8,)), dma((4,)), dma((4,)), dma((4,)), dma((4,)),
            dma((owners,)), dma((owners,)), dma((owners,)), dma((owners,)),
            dma((owners,)), dma((owners,)),
        ],
        compiler_params=pltpu.CompilerParams(
            collective_id=0, has_side_effects=True, vmem_limit_bytes=56 * 2**20),
        cost_estimate=pl.CostEstimate(
            flops=3 * 2 * 2**29, bytes_accessed=12 * 2**20, transcendentals=0),
    )(near_lists, stream, send, ids,
      inductance.reshape(leaf_count, near_count, 2, leaf_cells, leaf_cells))

    filament_voltage = lax.dot_general(
        placement, returned.reshape(slot_count, port_count), (((0,), (0,)), ((), ())),
        preferred_element_type=F32).astype(BF)
    return (loop_rows.transpose(1, 0, 2), filament_voltage)


def solution(mesh):
    return jax.shard_map(
        body,
        mesh=mesh,
        in_specs=(
            P("groups", "gx", "gy"),
            P(("groups", "gx"), ("gy", "gz"), None, None, None, None),
            P(("groups", "gx"), ("gy", "gz"), None),
            P(("groups", "gx", "gy", "gz")),
            P(("groups", "gx", "gy", "gz"), None),
            P(("groups", "gx", "gy", "gz"), None, None),
        ),
        out_specs=(P("groups", "gx", ("gy", "gz")), P(("groups", "gx", "gy", "gz"), None)),
        check_vma=False,
    )
```

```python
import functools

import jax
import jax.numpy as jnp
from jax import lax
from jax.experimental import pallas as pl
from jax.experimental.pallas import tpu as pltpu
from jax.sharding import PartitionSpec as P

LEAF_R = 8
LEAF_C = 16
LANES = 128
BF = jnp.bfloat16
F32 = jnp.float32


def exchange_blocks(values):
    lane_block = lax.broadcasted_iota(jnp.int32, values[0].shape, 1) // LEAF_C
    values = list(values)
    for bit in (1, 2, 4):
        low = (lane_block & bit) == 0
        shift = bit * LEAF_C
        for r in range(LEAF_R):
            if r & bit:
                continue
            a, b = values[r], values[r | bit]
            values[r] = jnp.where(low, a, pltpu.roll(b, shift, 1))
            values[r | bit] = jnp.where(low, pltpu.roll(a, LANES - shift, 1), b)
    return values


def sides(mid, before, after):
    lane = lax.broadcasted_iota(jnp.int32, mid.shape, 1)
    left = jnp.where(lane == 0, before, pltpu.roll(mid, 1, 1))
    right = jnp.where(lane == LANES - 1, after, pltpu.roll(mid, LANES - 1, 1))
    return left, right


CHUNK = 32


def kernel(
    dims, near_ref, tile_ref, slot_ref, coupling_ref, current_ref, ids_ref, ind_hbm, loop_ref, ret_ref,
    send_ref, stream_ref, bordered, planes, got, got_ids, ind, acc, ret_send, grid,
    col_out, row_in, col_in, frow_out, fcol_out, frow_in, fcol_in,
    ind_sem, halo_send, halo_recv, edge_send, edge_recv, fedge_send, fedge_recv,
    block_send, block_recv, id_send, id_recv, ret_ssem, ret_rsem,
):
    nx, ny, nz = dims
    nyz = ny * nz
    owners = nx * nyz
    leaf_rows, leaf_cols = bordered.shape[0] - 2, bordered.shape[1] - 2
    leaf_count = leaf_rows * leaf_cols
    ports, row_count = tile_ref.shape[:2]
    near_count = ind.shape[1]
    cap = send_ref.shape[1]
    mx, my, mz = lax.axis_index("gx"), lax.axis_index("gy"), lax.axis_index("gz")
    mc = my * nz + mz
    me = mx * nyz + mc
    mesh_id = pl.DeviceIdType.MESH

    def device(x, c):
        return {"gx": x, "gy": c // nz, "gz": c % nz}

    def peer(d):
        return device(d // nyz, d % nyz)

    def inside(dx, dc):
        x, c = mx + dx, mc + dc
        return (x >= 0) & (x < nx) & (c >= 0) & (c < nyz)

    ind_copy = pltpu.make_async_copy(ind_hbm, ind, ind_sem)
    ind_copy.start()
    barrier = pltpu.get_barrier_semaphore()

    @pl.loop(1, owners)
    def _(k):
        pl.semaphore_signal(
            barrier, inc=1, device_id=peer((me + k) % owners), device_id_type=mesh_id)

    lane = lax.broadcasted_iota(jnp.int32, (CHUNK, LANES), 1)

    def chunk(q):
        return pl.ds(pl.multiple_of(q * CHUNK, CHUNK), CHUNK)

    def gather_columns(source, target):
        @pl.loop(0, ports // CHUNK)
        def _(q):
            for side, at in ((0, 0), (1, LANES - 1)):
                total = jnp.zeros((CHUNK, LANES), F32)
                for x in range(row_count):
                    total = jnp.where(lane == x, source[x, chunk(q)][:, at:at + 1], total)
                target[side, chunk(q)] = total.astype(target.dtype)

    steps = ((-1, 0, 0, 1), (1, 0, 1, 0), (0, -1, 0, 1), (0, 1, 1, 0))

    def edge(number, first_row, last_row, col_from, row_to, col_to, ssem, rsem):
        dx, dc, mine, theirs = steps[number]
        if dx:
            src, dst = (last_row if mine else first_row), row_to.at[theirs]
        else:
            src, dst = col_from.at[mine], col_to.at[theirs]
        return pltpu.make_async_remote_copy(
            src_ref=src, dst_ref=dst, send_sem=ssem.at[number], recv_sem=rsem.at[number],
            device_id=device(mx + dx, mc + dc), device_id_type=mesh_id)

    def stream_edge(number):
        return edge(number, stream_ref.at[0], stream_ref.at[row_count - 1], col_out, row_in, col_in,
                    edge_send, edge_recv)

    def field_edge(number):
        return edge(number, frow_out.at[0], frow_out.at[1], fcol_out, frow_in, fcol_in,
                    fedge_send, fedge_recv)

    every_r, every_c = pl.ds(1, leaf_rows), pl.ds(1, leaf_cols)
    plans = []
    for dx in (-1, 0, 1):
        for dc in (-1, 0, 1):
            if dx or dc:
                src_r = every_r if dx == 0 else pl.ds(1 if dx < 0 else leaf_rows, 1)
                dst_r = every_r if dx == 0 else pl.ds(leaf_rows + 1 if dx < 0 else 0, 1)
                src_c = every_c if dc == 0 else pl.ds(1 if dc < 0 else leaf_cols, 1)
                dst_c = every_c if dc == 0 else pl.ds(leaf_cols + 1 if dc < 0 else 0, 1)
                plans.append((dx, dc, src_r, src_c, dst_r, dst_c))

    def halo(number):
        dx, dc, src_r, src_c, dst_r, dst_c = plans[number]
        return pltpu.make_async_remote_copy(
            src_ref=bordered.at[src_r, src_c], dst_ref=bordered.at[dst_r, dst_c],
            send_sem=halo_send.at[number], recv_sem=halo_recv.at[number],
            device_id=device(mx + dx, mc + dc), device_id_type=mesh_id)

    def over(moves, test_sign, action):
        for number, move in enumerate(moves):
            @pl.when(inside(test_sign * move[0], test_sign * move[1]))
            def _():
                action(number)

    def exchange(src, dst, ssem, rsem, d, slot):
        return pltpu.make_async_remote_copy(
            src_ref=src.at[d], dst_ref=dst.at[slot], send_sem=ssem.at[d], recv_sem=rsem.at[slot],
            device_id=peer(d), device_id_type=mesh_id)

    group = 2 * LANES
    group_owners = group // cap

    @pl.loop(0, owners // group_owners)
    def _(g):
        row = lax.broadcasted_iota(jnp.int32, (group, slot_ref.shape[1]), 0) + g * group
        mask = jnp.where(row == slot_ref[...], 1.0, 0.0).astype(BF)
        to = pl.ds(g * group_owners, group_owners)
        coupled = jnp.dot(mask, coupling_ref[...], preferred_element_type=F32).astype(BF)
        driven = jnp.dot(mask, current_ref[...], preferred_element_type=F32).astype(BF)
        send_ref[to, :, : 2 * LANES] = coupled.reshape(group_owners, cap, 2 * LANES)
        send_ref[to, :, 2 * LANES:] = driven.reshape(group_owners, cap, LANES)

    own_cols = pl.ds(pl.multiple_of(mz * LANES, LANES), LANES)

    @pl.loop(0, ports // CHUNK)
    def _(q):
        for x in range(row_count):
            stream_ref[x, chunk(q)] = tile_ref[chunk(q), x, own_cols]

    gather_columns(stream_ref, col_out)
    for number, (dx, dc, _, theirs) in enumerate(steps):
        @pl.when(jnp.logical_not(inside(-dx, -dc)))
        def _():
            for target in ((row_in, frow_in) if dx else (col_in, fcol_in)):
                target[theirs] = jnp.zeros(target.shape[1:], target.dtype)
    for dx, dc, _, _, dst_r, dst_c in plans:
        @pl.when(jnp.logical_not(inside(-dx, -dc)))
        def _():
            view = bordered.at[dst_r, dst_c]
            view[...] = jnp.zeros(view.shape, BF)

    pl.semaphore_wait(barrier, owners - 1)

    over(steps, 1, lambda number: stream_edge(number).start())

    def send_blocks(k):
        to = (mx + nx - k) % nx * nyz

        @pl.loop(1 if isinstance(k, int) and k == 0 else 0, nyz)
        def _(i):
            d = to + (mc + i) % nyz
            exchange(ids_ref, got_ids, id_send, id_recv, d, me).start()
            exchange(send_ref, got, block_send, block_recv, d, me).start()

    far = nx // 2
    send_blocks(0)
    if far:
        send_blocks(far)

    got[me] = send_ref[me]
    got_ids[me] = ids_ref[me]

    over(steps, -1, lambda number: stream_edge(number).wait_recv())

    for lr in range(leaf_rows):
        @pl.loop(0, ports // CHUNK)
        def _(q):
            def row(x):
                if x < 0:
                    return row_in[0, chunk(q)]
                if x >= row_count:
                    return row_in[1, chunk(q)]
                return stream_ref[x, chunk(q)]

            before, after = col_in[0, chunk(q)], col_in[1, chunk(q)]
            along_y, along_x = [], []
            for x in range(lr * LEAF_R, (lr + 1) * LEAF_R):
                left, right = sides(row(x), before[:, x:x + 1], after[:, x:x + 1])
                along_y.append(right - left)
                along_x.append(row(x - 1) - row(x + 1))
            for c, values in enumerate((along_y, along_x)):
                for j, value in enumerate(exchange_blocks(values)):
                    rounded = value.astype(BF)
                    bordered[lr + 1, j + 1, c, chunk(q)] = rounded
                    at = pl.multiple_of((lr * leaf_cols + j) * ports + q * CHUNK, CHUNK)
                    planes[pl.ds(at, CHUNK), c * LANES:(c + 1) * LANES] = rounded

    over(plans, 1, lambda number: halo(number).start())

    def over_rest(action):
        pl.loop(1, far)(action)
        pl.loop(far + 1, nx)(action)

    over_rest(send_blocks)

    per_row = LANES // cap
    width = nyz * cap
    stack = 4
    tall = stack * ports

    def work_on_blocks(k):
        first = isinstance(k, int) and k == 0
        base = (mx + k) % nx * nyz

        @pl.loop(1 if first else 0, nyz)
        def _(i):
            s = base + (mc + i) % nyz
            exchange(ids_ref, got_ids, id_send, id_recv, s, s).wait_recv()
            exchange(send_ref, got, block_send, block_recv, s, s).wait_recv()

        rows = []
        for g in range(nyz // per_row):
            total = got_ids[base + g * per_row]
            for o in range(1, per_row):
                total = total + got_ids[base + g * per_row + o]
            rows.append(total)
        ids_row = jnp.concatenate(rows, axis=1) - 1.0
        block = got[pl.ds(base, nyz)]
        coupling = block[:, :, : 2 * LANES].reshape(width, 2 * LANES)
        current_t = block[:, :, 2 * LANES:].reshape(width, LANES).astype(F32).T.astype(BF)

        volt = jnp.zeros((ports, width), F32)
        for b in range(leaf_count // stack):
            part = lax.dot_general(
                planes[b * tall:(b + 1) * tall, :], coupling, (((1,), (1,)), ((), ())),
                preferred_element_type=F32)
            for i in range(stack):
                hit = ids_row == float(b * stack + i)
                volt = volt + jnp.where(hit, part[i * ports:(i + 1) * ports], 0.0)
        ret_send[pl.ds(base, nyz)] = volt.T.astype(BF).reshape(nyz, cap, LANES)

        @pl.loop(1 if first else 0, nyz)
        def _(i):
            d = base + (mc + i) % nyz
            exchange(ret_send, ret_ref, ret_ssem, ret_rsem, d, me).start()

        for b in range(leaf_count // stack):
            masked = jnp.concatenate(
                [jnp.where(ids_row == float(b * stack + i), current_t, jnp.zeros((), BF))
                 for i in range(stack)], axis=0)
            part = jnp.dot(masked, coupling, preferred_element_type=F32)
            if first:
                acc[b * tall:(b + 1) * tall, :] = part
            else:
                acc[b * tall:(b + 1) * tall, :] += part

    work_on_blocks(0)
    ret_ref[me] = ret_send[me]
    if far:
        work_on_blocks(far)

    over(plans, -1, lambda number: halo(number).wait_recv())
    ind_copy.wait()

    @pl.loop(0, leaf_count)
    def _(l):
        r, j = l // leaf_cols, l % leaf_cols
        codes = [near_ref[r, j, n] for n in range(near_count)]
        at = pl.ds(pl.multiple_of(l * ports, ports), ports)
        for c in range(2):
            sources = jnp.concatenate(
                [bordered[r + code // 3, j + code % 3, c] for code in codes], axis=1)
            tiles = jnp.concatenate([ind[l, n, c] for n in range(near_count)], axis=1)
            acc[at, c * LANES:(c + 1) * LANES] += lax.dot_general(
                sources, tiles, (((1,), (1,)), ((), ())), preferred_element_type=F32)

    over_rest(work_on_blocks)

    for lr in range(leaf_rows):
        for c in range(2):
            @pl.loop(0, ports // CHUNK)
            def _(q):
                values = []
                for j in range(leaf_cols):
                    at = pl.multiple_of((lr * leaf_cols + j) * ports + q * CHUNK, CHUNK)
                    value = acc[pl.ds(at, CHUNK), c * LANES:(c + 1) * LANES]
                    values.append(value.astype(BF).astype(F32))
                for r, value in enumerate(exchange_blocks(values)):
                    grid[c, lr * LEAF_R + r, chunk(q)] = value

    frow_out[0] = grid[1, 0].astype(BF)
    frow_out[1] = grid[1, row_count - 1].astype(BF)
    gather_columns(grid.at[0], fcol_out)
    over(steps, 1, lambda number: field_edge(number).start())
    over(steps, -1, lambda number: field_edge(number).wait_recv())

    @pl.loop(0, ports // CHUNK)
    def _(q):
        def row(x):
            if x < 0:
                return frow_in[0, chunk(q)].astype(F32)
            if x >= row_count:
                return frow_in[1, chunk(q)].astype(F32)
            return grid[1, x, chunk(q)]

        before, after = fcol_in[0, chunk(q)].astype(F32), fcol_in[1, chunk(q)].astype(F32)
        for x in range(row_count):
            left, right = sides(grid[0, x, chunk(q)], before[:, x:x + 1], after[:, x:x + 1])
            loop_ref[x, chunk(q)] = (left - right) + (row(x + 1) - row(x - 1))

    @pl.loop(1, owners)
    def _(k):
        s = (me + k) % owners
        exchange(ids_ref, got_ids, id_send, id_recv, s, s).wait_send()
        exchange(send_ref, got, block_send, block_recv, s, s).wait_send()
        exchange(ret_send, ret_ref, ret_ssem, ret_rsem, s, s).wait()

    over(steps, 1, lambda number: stream_edge(number).wait_send())
    over(steps, 1, lambda number: field_edge(number).wait_send())
    over(plans, 1, lambda number: halo(number).wait_send())


def body(stream, inductance, near_lists, filament_leaf, filament_current, filament_coupling):
    port_count = stream.shape[0]
    leaf_rows, leaf_cols, near_count, _, leaf_cells, _ = inductance.shape
    leaf_count = leaf_rows * leaf_cols
    nx, ny, nz = lax.axis_size("gx"), lax.axis_size("gy"), lax.axis_size("gz")
    owners = nx * ny * nz
    me = (lax.axis_index("gx") * ny + lax.axis_index("gy")) * nz + lax.axis_index("gz")

    row_count = stream.shape[1]
    filament_count = filament_leaf.shape[0]
    capacity = max(16, 2 * filament_count // owners)
    slot_count = owners * capacity
    plane_cols = leaf_cols * ny * nz
    leaf_row = filament_leaf // plane_cols
    leaf_col = filament_leaf % plane_cols
    owner_ids = leaf_row // leaf_rows * (ny * nz) + leaf_col // leaf_cols
    local_ids = leaf_row % leaf_rows * leaf_cols + leaf_col % leaf_cols
    owner_hits = owner_ids[:, None] == jnp.arange(owners, dtype=jnp.int32)[None, :]
    numbers = jnp.arange(filament_count, dtype=jnp.int32)
    earlier = (numbers[None, :] < numbers[:, None]).astype(BF)
    ranks = jnp.dot(earlier, owner_hits.astype(BF), preferred_element_type=F32)
    position = jnp.sum(jnp.where(owner_hits, ranks, 0.0), axis=1).astype(jnp.int32)
    target_slot = owner_ids * capacity + position
    placement_mask = target_slot[None, :] == jnp.arange(slot_count, dtype=jnp.int32)[:, None]
    placement = placement_mask.astype(BF)
    sent_leaf = jnp.max(jnp.where(placement_mask, local_ids[None, :] + 1, 0), axis=1).astype(F32)
    per_row = LANES // capacity
    lane_part = (jnp.arange(per_row, dtype=jnp.int32) == me % per_row).astype(F32)
    ids = (sent_leaf.reshape(owners, 1, capacity) * lane_part[None, :, None]).reshape(owners, 1, LANES)

    vmem = pl.BlockSpec(memory_space=pltpu.VMEM)
    dma = pltpu.SemaphoreType.DMA
    tile = (port_count, LANES)
    block_shape = (owners, capacity, 2 * leaf_cells + port_count)
    loop_rows, returned = pl.pallas_call(
        functools.partial(kernel, (nx, ny, nz)),
        out_shape=(
            jax.ShapeDtypeStruct((row_count,) + tile, F32),
            jax.ShapeDtypeStruct((owners, capacity, port_count), BF),
        ),
        in_specs=[pl.BlockSpec(memory_space=pltpu.SMEM), vmem, vmem, vmem, vmem, vmem,
                  pl.BlockSpec(memory_space=pl.ANY)],
        out_specs=(vmem, vmem),
        scratch_shapes=[
            pltpu.VMEM(block_shape, BF),
            pltpu.VMEM((row_count,) + tile, F32),
            pltpu.VMEM((leaf_rows + 2, leaf_cols + 2, 2, port_count, leaf_cells), BF),
            pltpu.VMEM((leaf_count * port_count, 2 * leaf_cells), BF),
            pltpu.VMEM(block_shape, BF),
            pltpu.VMEM(ids.shape, F32),
            pltpu.VMEM((leaf_count, near_count, 2, leaf_cells, leaf_cells), BF),
            pltpu.VMEM((leaf_count * port_count, 2 * leaf_cells), F32),
            pltpu.VMEM((owners, capacity, port_count), BF),
            pltpu.VMEM((2, row_count) + tile, F32),
            pltpu.VMEM((2,) + tile, F32), pltpu.VMEM((2,) + tile, F32), pltpu.VMEM((2,) + tile, F32),
            pltpu.VMEM((2,) + tile, BF), pltpu.VMEM((2,) + tile, BF),
            pltpu.VMEM((2,) + tile, BF), pltpu.VMEM((2,) + tile, BF),
            dma, dma((8,)), dma((8,)), dma((4,)), dma((4,)), dma((4,)), dma((4,)),
            dma((owners,)), dma((owners,)), dma((owners,)), dma((owners,)),
            dma((owners,)), dma((owners,)),
        ],
        compiler_params=pltpu.CompilerParams(
            collective_id=0, has_side_effects=True, vmem_limit_bytes=56 * 2**20),
        cost_estimate=pl.CostEstimate(
            flops=3 * 2 * 2**29, bytes_accessed=12 * 2**20, transcendentals=0),
    )(near_lists, stream, target_slot.reshape(1, filament_count),
      filament_coupling.reshape(filament_count, 2 * leaf_cells), filament_current, ids,
      inductance.reshape(leaf_count, near_count, 2, leaf_cells, leaf_cells))

    filament_voltage = lax.dot_general(
        placement, returned.reshape(slot_count, port_count), (((0,), (0,)), ((), ())),
        preferred_element_type=F32).astype(BF)
    return (loop_rows.transpose(1, 0, 2), filament_voltage)


def solution(mesh):
    return jax.shard_map(
        body,
        mesh=mesh,
        in_specs=(
            P("groups", "gx", "gy"),
            P(("groups", "gx"), ("gy", "gz"), None, None, None, None),
            P(("groups", "gx"), ("gy", "gz"), None),
            P(("groups", "gx", "gy", "gz")),
            P(("groups", "gx", "gy", "gz"), None),
            P(("groups", "gx", "gy", "gz"), None, None),
        ),
        out_specs=(P("groups", "gx", ("gy", "gz")), P(("groups", "gx", "gy", "gz"), None)),
        check_vma=False,
    )
```
